32 devices in a mesh: section: 2 (over core), dp: 16 (over z, y, x).
Axes of the slice: x: 2, y: 2, z: 4, core: 2. Of those that a mesh axis runs over, the one named last changes fastest.
Arguments:
- inputs: bfloat16 [2, 16, 128, 768], P(None, 'dp'), may hold values from -6 to 6
- cotangent: bfloat16 [2, 16, 128, 768], P(None, 'dp'), may hold values from -6 to 6
- lengths: int32 [2, 16], P(None, 'dp'), may hold values from 32 to 128, as said below
- vectors: float32 [2, 768, 11], P('section'), as said below
- att_receptance: bfloat16 [2, 768, 768], P('section'), may hold values from -0.21875 to 0.21875
- att_key: bfloat16 [2, 768, 768], P('section'), may hold values from -0.21875 to 0.21875
- att_value: bfloat16 [2, 768, 768], P('section'), may hold values from -0.21875 to 0.21875
- att_output: bfloat16 [2, 768, 768], P('section'), may hold values from -0.875 to 0.875
- ffn_key: bfloat16 [2, 768, 3072], P('section'), may hold values from -0.21875 to 0.21875
- ffn_value: bfloat16 [2, 3072, 768], P('section'), may hold values from -0.21875 to 0.21875
- ffn_receptance: bfloat16 [2, 768, 768], P('section'), may hold values from -0.21875 to 0.21875
Outputs:
- acts: bfloat16 [2, 2, 16, 128, 768], P('section', None, 'dp')
- act_grads: float32 [2, 2, 16, 128, 768], P('section', None, 'dp')
- vectors_grad: float32 [2, 768, 11], P('section', 'dp')
- att_receptance_grad: float32 [2, 768, 768], P('section', 'dp')
- att_key_grad: float32 [2, 768, 768], P('section', 'dp')
- att_value_grad: float32 [2, 768, 768], P('section', 'dp')
- att_output_grad: float32 [2, 768, 768], P('section', 'dp')
- ffn_key_grad: float32 [2, 768, 3072], P('section', 'dp')
- ffn_value_grad: float32 [2, 3072, 768], P('section', 'dp')
- ffn_receptance_grad: float32 [2, 768, 768], P('section', 'dp')
The draws below stay inside these ranges and needn't reach their ends.
Inputs may be any that keep to these rules, and one draw needn't show every extreme that they name: `lengths`: in each micro-batch one sequence, drawn from the seed, has exactly 128 tokens; the others have 32 to 128, short ones more often than long ones. `vectors`: columns 0 and 2 lie in 0.5 to 1.5; columns 4, 5, 6, 9, 10 in 0.1 to 0.9; column 7 in log(0.5 / 128) to log(0.5); column 8 in -1 to 1; columns 1 and 3 are of order 0.3.
All inputs are finite; a program needn't handle non-finite values.
Results may differ from the reference program's by a relative error of at most 0.015.
Values may be sent and summed in bfloat16 or wider, within the bound.
A program may use at most 256 MiB of HBM per device.

```python
import math
import jax
import jax.numpy as jnp
from jax import lax

D = 768
FF = 3072
SLOT = 128
STRETCH = 128
MB = 2
LAYERS = 2
SEQS = 16
LMIN = 32


def draw_lengths(key, part):
    key = jax.random.fold_in(key, 11)
    key_power, key_extra, key_long = jax.random.split(key, 3)
    span_len = SLOT - LMIN
    shift_power = jax.random.randint(key_power, (MB, SEQS), 0, 4)
    reach = jnp.right_shift(jnp.full((MB, SEQS), span_len, jnp.int32), shift_power) + 1
    extra_len = jax.random.randint(key_extra, (MB, SEQS), 0, reach)
    longest = jax.random.randint(key_long, (MB, 1), 0, SEQS)
    places = jnp.arange(SEQS, dtype=jnp.int32)[None, :]
    return jnp.where(places == longest, SLOT, LMIN + extra_len).astype(jnp.int32)


def draw_vectors(key, part):
    key = jax.random.fold_in(key, 23)
    key_gain, key_bias, key_mix, key_rest = jax.random.split(key, 4)
    amplitude_rows = jax.random.uniform(key_gain, (LAYERS, D, 2), jnp.float32, 0.5, 1.5)
    offset_rows = 0.3 * jax.random.normal(key_bias, (LAYERS, D, 2), jnp.float32)
    blend_coefficients = jax.random.uniform(key_mix, (LAYERS, D, 5), jnp.float32, 0.1, 0.9)
    equal_portion = jax.random.uniform(key_rest, (LAYERS, D, 2), jnp.float32, 0.0, 1.0)
    lowest = math.log(0.5 / SLOT)
    fading_multiplier = lowest + equal_portion[..., 0:1] * (math.log(0.5) - lowest)
    reward_entries = 2.0 * equal_portion[..., 1:2] - 1.0
    return jnp.concatenate([amplitude_rows[..., 0:1], offset_rows[..., 0:1], amplitude_rows[..., 1:2], offset_rows[..., 1:2], blend_coefficients[..., 0:3], fading_multiplier, reward_entries, blend_coefficients[..., 3:5]], axis=-1)


def raised(array, own_key, source, target, blocks, factor):
    def block_of(axis_at):
        return (jnp.arange(array.shape[axis_at]) // (array.shape[axis_at] // blocks)).reshape((-1,) + (1,) * (array.ndim - 1 - axis_at))

    one_side = jax.random.permutation(own_key, blocks)[block_of(target)]
    far = (block_of(target) + blocks // 2) % blocks
    return jnp.where((block_of(source) == one_side) | (block_of(source) == far), factor * array, array)


def level_of(key, shape, cuts, least, largest):
    def one(axis_at, blocks):
        steps = jax.random.uniform(jax.random.fold_in(jax.random.fold_in(key, 6), axis_at), (blocks,), jnp.float32, least / len(cuts), largest / len(cuts))
        return jnp.repeat(jnp.exp(steps), shape[axis_at] // blocks).reshape((-1,) + (1,) * (len(shape) - axis_at - 1))

    level = one(*cuts[0])
    for cut in cuts[1:]:
        level = level * one(*cut)
    return level


def noise(key, extent, deviation, bound, cuts=(), held_as=jnp.bfloat16):
    gain = level_of(key, extent, cuts, -0.22, 0.18) if cuts else 1.0
    array = jax.random.normal(key, extent, jnp.float32) * deviation * gain
    return jnp.minimum(jnp.maximum(array, -bound), bound).astype(held_as)


def heavy_noise(own_key, extent, scale, limit, cuts, heavy, kind=jnp.bfloat16):
    array = scale * jax.random.normal(own_key, extent, jnp.float32)
    if cuts:
        array = array * level_of(own_key, extent, cuts, -0.22, 0.18)
    return jnp.clip(raised(array, jax.random.fold_in(own_key, 3), *heavy), -limit, limit).astype(kind)


def setup_inputs(seed: int = 0) -> dict:
    arg_keys = jax.random.split(jax.random.key(seed), 12)
    return {
        "inputs": noise(arg_keys[0], (MB, SEQS, SLOT, D), 1.0, 6.0, ((1, 16),)),
        "cotangent": heavy_noise(arg_keys[1], (MB, SEQS, SLOT, D), 1.0, 6.0, ((1, 16),), (1, 3, 16, 2.0)),
        "lengths": draw_lengths(jax.random.fold_in(arg_keys[11], 71), 0),
        "vectors": draw_vectors(jax.random.fold_in(arg_keys[11], 71), 0),
        "att_receptance": noise(arg_keys[4], (LAYERS, D, D), D ** -0.5, 0.21875, ((0, 2),)),
        "att_key": noise(arg_keys[5], (LAYERS, D, D), D ** -0.5, 0.21875, ((0, 2),)),
        "att_value": noise(arg_keys[6], (LAYERS, D, D), D ** -0.5, 0.21875, ((0, 2),)),
        "att_output": noise(arg_keys[7], (LAYERS, D, D), (D // 16) ** -0.5, 0.875, ((0, 2),)),
        "ffn_key": noise(arg_keys[8], (LAYERS, D, FF), D ** -0.5, 0.21875, ((0, 2),)),
        "ffn_value": noise(arg_keys[9], (LAYERS, FF, D), (FF // 4) ** -0.5, 0.21875, ((0, 2),)),
        "ffn_receptance": noise(arg_keys[10], (LAYERS, D, D), D ** -0.5, 0.21875, ((0, 2),)),
    }


@jax.custom_vjp
def low(v):
    return lax.optimization_barrier(v.astype(jnp.bfloat16)).astype(jnp.float32)

@jax.custom_vjp
def low_back(v):
    return v

def low_keep(v):
    return (low(v), None)

def low_pass(kept, grad):
    return (grad,)

def back_keep(v):
    return (v, None)

def back_low(kept, grad):
    return (low(grad),)
low.defvjp(low_keep, low_pass)
low_back.defvjp(back_keep, back_low)
highest = lax.Precision.HIGHEST

def layer_norm(stream, gain_row, bias_row):
    centred = stream - lax.optimization_barrier(jnp.mean(stream, axis=-1, keepdims=True))
    spread = lax.optimization_barrier(jnp.mean(centred * centred, axis=-1, keepdims=True))
    return centred * lax.rsqrt(spread + 1e-05) * gain_row + bias_row

def shifted(stream):
    return jnp.concatenate([jnp.zeros_like(stream[:1]), stream[:-1]], axis=0)

def blend(present_element, earlier, fraction):
    return present_element * fraction + earlier * (1.0 - fraction)

def stretched_lookups(mapped_lookups, mapped_payloads, fading_pace, initial_element_reward, segment_extent):
    seq_len, features = mapped_lookups.shape
    offsets = jnp.arange(segment_extent, dtype=mapped_lookups.dtype)[:, None]
    lower = (jnp.arange(segment_extent)[:, None] > jnp.arange(segment_extent)[None, :]).astype(mapped_lookups.dtype)
    growth = jnp.exp(offsets * fading_pace)
    shrink = jnp.exp(-(offsets - 1.0) * fading_pace)
    fading = jnp.exp(-offsets * fading_pace)
    carry_decay = jnp.exp(-segment_extent * fading_pace)
    carry_scale = jnp.exp(-(segment_extent - 1.0) * fading_pace)

    def advance(state, pieces):
        numerator, denominator = state
        segment_lookups, value_block = pieces
        factor = jnp.exp(segment_lookups) * growth
        joined = jnp.concatenate([factor * value_block, factor], axis=1)
        before = jnp.dot(lower, joined, precision=highest)
        totals = lax.optimization_barrier(jnp.sum(joined, axis=0))
        present_element = jnp.exp(initial_element_reward + segment_lookups)
        top_sum = fading * numerator + shrink * before[:, :features] + present_element * value_block
        bottom_sum = fading * denominator + shrink * before[:, features:] + present_element
        state = (carry_decay * numerator + carry_scale * totals[:features], carry_decay * denominator + carry_scale * totals[features:])
        return (state, top_sum / bottom_sum)
    empty_state = jnp.zeros((features,), mapped_lookups.dtype)
    split_blocks = (mapped_lookups.reshape(seq_len // segment_extent, segment_extent, features), mapped_payloads.reshape(seq_len // segment_extent, segment_extent, features))
    _, result = lax.scan(jax.checkpoint(advance), (empty_state, empty_state), split_blocks)
    return result.reshape(seq_len, features)

def product(left_side, right_side):
    return jnp.dot(left_side, right_side, precision=highest)

def layer(stream, vector_table, matrices, masking):
    receptance, key_weight, value_weight, out_weight, feed_kweight, feed_vweight, feed_rweight = matrices
    normed = layer_norm(stream, vector_table[:, 0], vector_table[:, 1])
    earlier = shifted(normed)
    mix_key = low(blend(normed, earlier, vector_table[:, 4]))
    mix_value = low(blend(normed, earlier, vector_table[:, 5]))
    mix_recept = low(blend(normed, earlier, vector_table[:, 6]))
    mapped_lookups = low_back(product(mix_key, key_weight))
    mapped_payloads = low_back(product(mix_value, value_weight))
    recept = low_back(product(mix_recept, receptance))
    mixture = jax.nn.sigmoid(recept) * stretched_lookups(mapped_lookups, mapped_payloads, jnp.exp(vector_table[:, 7]), vector_table[:, 8], STRETCH)
    mix_out = low(mixture)
    branch = low_back(product(mix_out, out_weight))
    middle = stream + branch
    normed_two = layer_norm(middle, vector_table[:, 2], vector_table[:, 3])
    later = shifted(normed_two)
    feed_key = low(blend(normed_two, later, vector_table[:, 9]))
    feed_recept = low(blend(normed_two, later, vector_table[:, 10]))
    hidden_pre = low_back(product(feed_key, feed_kweight))
    gate_pre = low_back(product(feed_recept, feed_rweight))
    hidden = low(jnp.square(jax.nn.relu(hidden_pre)))
    mapped = low_back(product(hidden, feed_vweight))
    return masking * (middle + jax.nn.sigmoid(gate_pre) * mapped)

def reference(inputs, cotangent, lengths, vectors, att_receptance, att_key, att_value, att_output, ffn_key, ffn_value, ffn_receptance):
    seq_count = MB * SEQS
    sequences = inputs.reshape(seq_count, SLOT, D).astype(jnp.float32)
    cot_rows = cotangent.reshape(seq_count, SLOT, D).astype(jnp.float32)
    seq_lengths = lengths.reshape(seq_count).astype(jnp.int32)
    matrices = tuple((weight.astype(jnp.float32) for weight in (att_receptance, att_key, att_value, att_output, ffn_key, ffn_value, ffn_receptance)))
    positions = jnp.arange(SLOT, dtype=jnp.int32)
    probe_grad = jnp.zeros_like(sequences)

    def forward(sequences, probe_grad, vectors, matrices):
        first_mats = tuple((matrix[0] for matrix in matrices))
        second_mats = tuple((matrix[1] for matrix in matrices))

        def one_sequence(pieces):
            sequence, offset_in, seq_size = pieces
            masking = (positions < seq_size).astype(sequence.dtype)[:, None]
            first_out = layer(sequence, vectors[0], first_mats, masking)
            passed = low_back(low(first_out)) + offset_in
            second_out = layer(passed, vectors[1], second_mats, masking)
            return (low(first_out), low(second_out))
        return lax.map(jax.checkpoint(one_sequence), (sequences, probe_grad, seq_lengths))
    (first_all, second_all), pullback = jax.vjp(forward, sequences, probe_grad, vectors, matrices)
    grad_seqs, grad_probe, grad_vectors, grad_mats = pullback((jnp.zeros_like(first_all), cot_rows))
    acts = jnp.stack([first_all, second_all]).reshape(LAYERS, MB, SEQS, SLOT, D).astype(jnp.bfloat16)
    act_grads = jnp.stack([grad_seqs, grad_probe]).reshape(LAYERS, MB, SEQS, SLOT, D).astype(jnp.float32)
    return (acts, act_grads, grad_vectors, grad_mats[0], grad_mats[1], grad_mats[2], grad_mats[3], grad_mats[4], grad_mats[5], grad_mats[6])
```

```python
import functools

import jax
import jax.numpy as jnp
from jax import lax
from jax.experimental import pallas as pl
from jax.experimental.pallas import tpu as pltpu
from jax.sharding import PartitionSpec as P

F32 = jnp.float32
BF16 = jnp.bfloat16
MESH = pl.DeviceIdType.MESH
LANES = 128
VROWS = 16
COLS = 11


def nn(left, right):
    return jnp.dot(left, right, preferred_element_type=F32)


def nt(left, right):
    return lax.dot_general(left, right, (((1,), (1,)), ((), ())), preferred_element_type=F32)


def tn(left, right):
    return lax.dot_general(left, right, (((0,), (0,)), ((), ())), preferred_element_type=F32)


def rows_iota(shape):
    return lax.broadcasted_iota(jnp.int32, shape, 0)


def shift_down(block):
    return jnp.where(rows_iota(block.shape) == 0, 0.0, pltpu.roll(block, 1, 0))


def shift_up(block):
    last = block.shape[0] - 1
    return jnp.where(rows_iota(block.shape) == last, 0.0, pltpu.roll(block, last, 0))


def two_parts(value):
    high = value.astype(BF16)
    low = (value - high.astype(F32)).astype(BF16)
    return jnp.concatenate([high, low], axis=0)


def colsum(value):
    return jnp.sum(value, axis=0, keepdims=True)


def layer_kernel(batches, places, features, hidden_size, *refs):
    (
        lengths, vec, inputs, cotangent, w_r, w_k, w_v, w_o, w_fk, w_fv, w_fr,
        acts, act_grads, vgrad, o_r, o_k, o_v, o_o, o_fk, o_fv, o_fr,
        b_r, b_k, b_v, b_o, b_fk, b_fv, b_fr,
        xin, gin, n1, rs1, n2, rs2, mixk, mixv, mixr, kp, vp, rp, ybuf, ibot, mixout, middle,
        feedk, feedr, hpre, hidden, mapped, sgate, yout, growth, shrink, masks,
        gmap, ggate, gpre, gbr, gkey, gval, grec, t1, t2, t3, gmid, gx, gxb, vg,
        g_r, g_k, g_v, g_o, g_fk, g_fv, g_fr,
        sem_w, sem_io, sem_out, sem_fs, sem_fr, sem_bs, sem_br,
    ) = refs
    sec = lax.axis_index("section")
    dp = lax.axis_index("dp")
    other = (1 - sec, dp)
    tokens = batches * places
    blocks = features // LANES

    weights = [(w_r, b_r), (w_k, b_k), (w_v, b_v), (w_o, b_o), (w_fk, b_fk), (w_fv, b_fv), (w_fr, b_fr)]
    loads = [pltpu.make_async_copy(src.at[0], dst, sem_w.at[i]) for i, (src, dst) in enumerate(weights)]
    in_loads = [
        pltpu.make_async_copy(inputs.at[m, 0], xin.at[pl.ds(m * places, places)], sem_io.at[0, m])
        for m in range(batches)
    ]
    cot_loads = [
        pltpu.make_async_copy(cotangent.at[m, 0], gin.at[pl.ds(m * places, places)], sem_io.at[1, m])
        for m in range(batches)
    ]

    @pl.when(sec == 0)
    def _():
        for load in in_loads:
            load.start()

    for i in (1, 2, 0, 3, 4, 6, 5):
        loads[i].start()

    @pl.when(sec == 1)
    def _():
        for load in cot_loads:
            load.start()

    barrier = pltpu.get_barrier_semaphore()
    pl.semaphore_signal(barrier, inc=1, device_id=other, device_id_type=MESH)

    place = rows_iota((places, LANES)).astype(F32)

    def tables(cb, _):
        cols = pl.ds(pl.multiple_of(cb * LANES, LANES), LANES)
        pace = jnp.exp(vec[7:8, cols])
        growth[:, cols] = jnp.exp(place * pace)
        shrink[:, cols] = jnp.exp(-(place - 1.0) * pace)
        return 0

    lax.fori_loop(0, blocks, tables, 0)
    vg[...] = jnp.zeros_like(vg)
    for m in range(batches):
        size = lengths[m, 0]
        masks[m * places:(m + 1) * places, :] = jnp.where(
            rows_iota((places, LANES)) < size, 1.0, 0.0
        ).astype(F32)
    row_id = lax.broadcasted_iota(jnp.int32, (places, 2 * places), 0)
    col_id = lax.broadcasted_iota(jnp.int32, (places, 2 * places), 1)
    col_id = jnp.where(col_id >= places, col_id - places, col_id)
    lower = jnp.where(row_id > col_id, 1.0, 0.0).astype(BF16)
    upper = jnp.where(row_id < col_id, 1.0, 0.0).astype(BF16)

    pl.semaphore_wait(barrier, 1)

    def norm_rows(source, base, count, normed, spread):
        def body(i, _):
            r = pl.ds(pl.multiple_of(base + i * 16, 16), 16)
            x = source[r, :].astype(F32)
            c = x - jnp.mean(x, axis=1, keepdims=True)
            s = lax.rsqrt(jnp.mean(c * c, axis=1, keepdims=True) + 1e-5)
            normed[r, :] = c * s
            spread[r, :] = s
            return 0

        lax.fori_loop(0, count // 16, body, 0, unroll=2)

    def each_block(mb_from, mb_to, body):
        def run(i, _):
            m = i // blocks
            cb = i - m * blocks
            rows = pl.ds(pl.multiple_of(m * places, places), places)
            cols = pl.ds(pl.multiple_of(cb * LANES, LANES), LANES)
            body(rows, cols)
            return 0

        lax.fori_loop(mb_from * blocks, mb_to * blocks, run, 0)

    forward_sends = [
        pltpu.make_async_remote_copy(
            src_ref=yout.at[pl.ds(m * places, places)],
            dst_ref=xin.at[pl.ds(m * places, places)],
            send_sem=sem_fs.at[m], recv_sem=sem_fr.at[m],
            device_id=other, device_id_type=MESH,
        )
        for m in range(batches)
    ]
    acts_out = [
        pltpu.make_async_copy(yout.at[pl.ds(m * places, places)], acts.at[0, m, 0], sem_out.at[0, m])
        for m in range(batches)
    ]
    grads_out = [
        pltpu.make_async_copy(gx.at[pl.ds(m * places, places)], act_grads.at[0, m, 0], sem_out.at[1, m])
        for m in range(batches)
    ]
    back_send = pltpu.make_async_remote_copy(
        src_ref=gxb, dst_ref=gin, send_sem=sem_bs, recv_sem=sem_br,
        device_id=other, device_id_type=MESH,
    )

    for m in range(batches):
        rows = pl.ds(m * places, places)

        @pl.when(sec == 0)
        def _():
            in_loads[m].wait()

        @pl.when(sec == 1)
        def _():
            forward_sends[m].wait_recv()

        norm_rows(xin, m * places, places, n1, rs1)

        def mix_first(rows, cols):
            a = n1[rows, cols] * vec[0:1, cols] + vec[1:2, cols]
            d = shift_down(a)
            for target, row in ((mixk, 4), (mixv, 5), (mixr, 6)):
                share = vec[row:row + 1, cols]
                target[rows, cols] = (a * share + d * (1.0 - share)).astype(BF16)

        each_block(m, m + 1, mix_first)
        if m == 0:
            loads[1].wait()
        kp[rows, :] = nn(mixk[rows, :], b_k[...])
        if m == 0:
            loads[2].wait()
        vp[rows, :] = nn(mixv[rows, :], b_v[...])
        if m == 0:
            loads[0].wait()
        rp[rows, :] = nn(mixr[rows, :], b_r[...])

        def wkv(rows, cols):
            e = jnp.exp(kp[rows, cols])
            v = vp[rows, cols]
            f = e * growth[:, cols]
            joined = jnp.concatenate([two_parts(f * v), two_parts(f)], axis=1)
            before = nn(lower, joined)
            p = e * jnp.exp(vec[8:9, cols])
            s = shrink[:, cols]
            inverse = 1.0 / (s * before[:, LANES:] + p)
            y = (s * before[:, :LANES] + p * v) * inverse
            ybuf[rows, cols] = y
            ibot[rows, cols] = inverse
            mixout[rows, cols] = (jax.nn.sigmoid(rp[rows, cols]) * y).astype(BF16)

        each_block(m, m + 1, wkv)
        if m == 0:
            loads[3].wait()
        middle[rows, :] = xin[rows, :].astype(F32) + nn(mixout[rows, :], b_o[...])
        norm_rows(middle, m * places, places, n2, rs2)

        def mix_second(rows, cols):
            a = n2[rows, cols] * vec[2:3, cols] + vec[3:4, cols]
            d = shift_down(a)
            for target, row in ((feedk, 9), (feedr, 10)):
                share = vec[row:row + 1, cols]
                target[rows, cols] = (a * share + d * (1.0 - share)).astype(BF16)

        each_block(m, m + 1, mix_second)
        if m == 0:
            loads[4].wait()
        step = 512
        for h in range(0, hidden_size, step):
            top = jnp.maximum(nn(feedk[rows, :], b_fk[:, h:h + step]), 0.0)
            hpre[rows, h:h + step] = top
            hidden[rows, h:h + step] = (top * top).astype(BF16)
        if m == 0:
            loads[6].wait()
        sgate[rows, :] = jax.nn.sigmoid(nn(feedr[rows, :], b_fr[...]))
        if m == 0:
            loads[5].wait()
        mapped[rows, :] = nn(hidden[rows, :], b_fv[...])

        def closing(rows, cols):
            y = masks[rows, :] * (middle[rows, cols] + sgate[rows, cols] * mapped[rows, cols])
            yout[rows, cols] = y.astype(BF16)

        each_block(m, m + 1, closing)

        @pl.when(sec == 0)
        def _():
            forward_sends[m].start()

        acts_out[m].start()

    @pl.when(sec == 0)
    def _():
        back_send.wait_recv()

    @pl.when(sec == 1)
    def _():
        for load in cot_loads:
            load.wait()

    def feed_start(rows, cols):
        up = masks[rows, :] * gin[rows, cols].astype(F32)
        s = sgate[rows, cols]
        gmap[rows, cols] = (up * s).astype(BF16)
        ggate[rows, cols] = (up * mapped[rows, cols] * s * (1.0 - s)).astype(BF16)

    each_block(0, batches, feed_start)
    step = 512
    for h in range(0, hidden_size, step):
        back = nt(gmap[...], b_fv[h:h + step, :])
        gpre[:, h:h + step] = (2.0 * hpre[:, h:h + step] * back).astype(BF16)
    step = 256
    for h in range(0, features, step):
        t1[:, h:h + step] = nt(gpre[...], b_fk[h:h + step, :])
        t2[:, h:h + step] = nt(ggate[...], b_fr[h:h + step, :])

    def back_second(rows, cols):
        n = n2[rows, cols]
        gain = vec[2:3, cols]
        a = n * gain + vec[3:4, cols]
        d = a - shift_down(a)
        one = t1[rows, cols]
        two = t2[rows, cols]
        first = vec[9:10, cols]
        second = vec[10:11, cols]
        grad = one * first + two * second + shift_up(one * (1.0 - first) + two * (1.0 - second))
        vg[9:10, cols] += colsum(one * d)
        vg[10:11, cols] += colsum(two * d)
        vg[2:3, cols] += colsum(grad * n)
        vg[3:4, cols] += colsum(grad)
        t1[rows, cols] = grad * gain

    each_block(0, batches, back_second)

    def rows_second(i, _):
        r = pl.ds(pl.multiple_of(i * 16, 16), 16)
        g = t1[r, :]
        n = n2[r, :]
        inner = g - jnp.mean(g, axis=1, keepdims=True) - n * jnp.mean(g * n, axis=1, keepdims=True)
        total = masks[r, 0:1] * gin[r, :].astype(F32) + rs2[r, :] * inner
        gmid[r, :] = total
        gbr[r, :] = total.astype(BF16)
        return 0

    lax.fori_loop(0, tokens // 16, rows_second, 0, unroll=2)
    for h in range(0, features, step):
        t1[:, h:h + step] = nt(gbr[...], b_o[h:h + step, :])

    def back_wkv(rows, cols):
        g = t1[rows, cols]
        s = jax.nn.sigmoid(rp[rows, cols])
        y = ybuf[rows, cols]
        v = vp[rows, cols]
        e = jnp.exp(kp[rows, cols])
        f = e * growth[:, cols]
        p = e * jnp.exp(vec[8:9, cols])
        grec[rows, cols] = (g * y * s * (1.0 - s)).astype(BF16)
        gtop = g * s * ibot[rows, cols]
        gnum = shrink[:, cols] * gtop
        joined = jnp.concatenate([two_parts(gnum), two_parts(-gnum * y)], axis=1)
        after = nn(upper, joined)
        ga = after[:, :LANES]
        ff = (ga * v + after[:, LANES:]) * f
        pg = gtop * (v - y) * p
        gkey[rows, cols] = (ff + pg).astype(BF16)
        gval[rows, cols] = (ga * f + gtop * p).astype(BF16)
        vg[8:9, cols] += colsum(pg)
        vg[7:8, cols] += jnp.exp(vec[7:8, cols]) * colsum(place * ff + (place - 1.0) * pg)

    each_block(0, batches, back_wkv)
    for h in range(0, features, step):
        t1[:, h:h + step] = nt(gkey[...], b_k[h:h + step, :])
        t2[:, h:h + step] = nt(gval[...], b_v[h:h + step, :])
        t3[:, h:h + step] = nt(grec[...], b_r[h:h + step, :])

    def back_first(rows, cols):
        n = n1[rows, cols]
        gain = vec[0:1, cols]
        a = n * gain + vec[1:2, cols]
        d = a - shift_down(a)
        grad = None
        for source, row in ((t1, 4), (t2, 5), (t3, 6)):
            value = source[rows, cols]
            share = vec[row:row + 1, cols]
            vg[row:row + 1, cols] += colsum(value * d)
            here, back = value * share, value * (1.0 - share)
            grad, behind = (here, back) if grad is None else (grad + here, behind + back)
        grad = grad + shift_up(behind)
        vg[0:1, cols] += colsum(grad * n)
        vg[1:2, cols] += colsum(grad)
        t1[rows, cols] = grad * gain

    each_block(0, batches, back_first)

    def rows_first(i, _):
        r = pl.ds(pl.multiple_of(i * 16, 16), 16)
        g = t1[r, :]
        n = n1[r, :]
        inner = g - jnp.mean(g, axis=1, keepdims=True) - n * jnp.mean(g * n, axis=1, keepdims=True)
        total = gmid[r, :] + rs1[r, :] * inner
        gx[r, :] = total
        gxb[r, :] = total.astype(BF16)
        return 0

    lax.fori_loop(0, tokens // 16, rows_first, 0, unroll=2)

    @pl.when(sec == 1)
    def _():
        back_send.start()

    for out in grads_out:
        out.start()

    pairs = [
        (mixr, grec, g_r), (mixk, gkey, g_k), (mixv, gval, g_v), (mixout, gbr, g_o),
        (feedk, gpre, g_fk), (hidden, gmap, g_fv), (feedr, ggate, g_fr),
    ]
    for left, right, target in pairs:
        step_m, step_n = 256, 768
        for i in range(0, left.shape[1], step_m):
            for j in range(0, right.shape[1], step_n):
                target[i:i + step_m, j:j + step_n] = tn(
                    left[:, i:i + step_m], right[:, j:j + step_n]
                ).astype(target.dtype)
    results = [
        pltpu.make_async_copy(src, dst, sem_w.at[i])
        for i, (src, dst) in enumerate(
            [(g_r, o_r), (g_k, o_k), (g_v, o_v), (g_o, o_o), (g_fk, o_fk), (g_fv, o_fv), (g_fr, o_fr)]
        )
    ]
    for out in results:
        out.start()
    vgrad[...] = vg[...]
    for out in results + acts_out + grads_out:
        out.wait()

    @pl.when(sec == 0)
    def _():
        for send in forward_sends:
            send.wait_send()

    @pl.when(sec == 1)
    def _():
        back_send.wait_send()


def per_device(inputs, cotangent, lengths, vectors, *weights):
    batches, _, places, features = inputs.shape
    hidden_size = weights[4].shape[2]
    tokens = batches * places
    vec = jnp.pad(vectors[0].T, ((0, VROWS - COLS), (0, 0)))
    hbm = pl.BlockSpec(memory_space=pl.ANY)
    vmem = pl.BlockSpec(memory_space=pltpu.VMEM)
    smem = pl.BlockSpec(memory_space=pltpu.SMEM)
    shapes = [w.shape[1:] for w in weights]

    def wide(kind, width=features):
        return pltpu.VMEM((tokens, width), kind)

    b, f = BF16, F32
    scratch = [pltpu.VMEM(s, b) for s in shapes]
    scratch += [wide(b), wide(b), wide(f), wide(f, 1), wide(f), wide(f, 1)]
    scratch += [wide(b)] * 3 + [wide(f)] * 5 + [wide(b), wide(f)]
    scratch += [wide(b)] * 2 + [wide(f, hidden_size), wide(b, hidden_size), wide(f), wide(f), wide(b)]
    scratch += [pltpu.VMEM((places, features), f)] * 2 + [wide(f, LANES)]
    scratch += [wide(b)] * 2 + [wide(b, hidden_size)] + [wide(b)] * 4
    scratch += [wide(f)] * 3 + [wide(f), wide(f), wide(b), pltpu.VMEM((VROWS, features), f)]
    scratch += [pltpu.VMEM(s, b) for s in shapes]
    dma = pltpu.SemaphoreType.DMA
    scratch += [dma((7,)), dma((2, batches)), dma((2, batches)), dma((batches,)), dma((batches,)), dma, dma]
    out_shape = [
        jax.ShapeDtypeStruct((1, batches, 1, places, features), BF16),
        jax.ShapeDtypeStruct((1, batches, 1, places, features), F32),
        jax.ShapeDtypeStruct((VROWS, features), F32),
    ] + [jax.ShapeDtypeStruct(s, BF16) for s in shapes]
    outs = pl.pallas_call(
        functools.partial(layer_kernel, batches, places, features, hidden_size),
        out_shape=out_shape,
        in_specs=[smem, vmem] + [hbm] * 9,
        out_specs=[hbm, hbm, vmem] + [hbm] * 7,
        scratch_shapes=scratch,
        compiler_params=pltpu.CompilerParams(
            collective_id=0, has_side_effects=True, vmem_limit_bytes=62 * 2**20
        ),
    )(lengths, vec, inputs, cotangent, *weights)
    acts, act_grads, vgrad = outs[:3]

    def share(value):
        return lax.psum_scatter(value.astype(F32), "dp", scatter_dimension=0, tiled=True)[None]

    grads = [share(g) for g in outs[3:]]
    return (acts, act_grads, share(vgrad.T[:, :COLS])) + tuple(grads)


def solution(mesh):
    token = P(None, "dp", None, None)
    weight = P("section", None, None)
    layered = P("section", None, "dp", None, None)
    grad = P("section", "dp", None)
    return jax.shard_map(
        per_device,
        mesh=mesh,
        in_specs=(token, token, P(None, "dp")) + (weight,) * 8,
        out_specs=(layered, layered) + (grad,) * 8,
        check_vma=False,
    )
```
